32 devices in a mesh: mem: 4 (over y, x), col: 8 (over z, core).
Axes of the slice: x: 2, y: 2, z: 4, core: 2. Of those that a mesh axis runs over, the one named last changes fastest.
Arguments:
- perturbations: bfloat16 [32, 32, 256, 128], P('mem', 'col'), may hold values from -4 to 4
- static_root: float32 [128, 128], replicated, may hold values from -0.5 to 1.5
- obs_jacobian: float32 [128, 128], replicated, may hold values from -0.5 to 0.5
- innovations: float32 [2048, 128], P('col'), may hold values from -6 to 6
- obs_weights: float32 [128], replicated, may hold values from 0.2 to 2
- length_scale: float32 [32, 256], P('col'), may hold values from 0.05 to 0.24
- obs_owner: int32 [2048, 1], P('col'), may hold values from 0 to 7; in each aligned block of 256 rows (0 to 255, 256 to 511, ...) at most 64 rows name the same one
- obs_cell: int32 [2048], P('col'), may hold values from 0 to 1023
- obs_count: int32 [8], P('col'), may hold values from 128 to 256, as said below
Outputs:
- increment: float32 [32, 256, 128], P('col', 'mem')
- control_static: float32 [32, 256, 128], P('col', 'mem')
- control_ensemble: float32 [32, 32, 256], P('mem', 'col')
The draws below stay inside these ranges and needn't reach their ends.
Inputs may be any that keep to these rules, and one draw needn't show every extreme that they name: `obs_owner`: each holder's 256 rows name any one column block at most 64 times. `obs_count`: rows at or past a holder's count are padding and are ignored; at least one holder is full. `obs_cell`: the column within the owner's block, numbered y * 256 + x, where y is its grid row within the block (0 to 3).
All inputs are finite; a program needn't handle non-finite values.
Results may differ from the reference program's by a relative error of at most 0.004.
Values may be sent and summed in bfloat16 or wider, within the bound.
A program may use at most 64 MiB of HBM per device.

```python
import math
import jax
import jax.numpy as jnp
import numpy as np
from jax import lax

FEAT = 128
CH = 128
MEMBERS = 32
CY = 4
NX = 256
NY = 32
OBS_DEV = 256
OBS_TOT = 2048
CAP = 64
NSWEEP = 4
ITERS = 2
N_COL = 8


def draw_static_root(key, part):
    first, second = jax.random.split(jax.random.fold_in(key, 11))
    diagonal = jax.random.uniform(first, (FEAT,), jnp.float32, 0.7, 1.3)
    spread = jnp.clip(jax.random.normal(second, (FEAT, FEAT), jnp.float32), -4.0, 4.0) * (0.5 / math.sqrt(FEAT))
    return jnp.eye(FEAT, dtype=jnp.float32) * diagonal[None, :] + spread


def draw_obs_count(key, part):
    first, second = jax.random.split(jax.random.fold_in(key, 23))
    counts = jax.random.randint(first, (N_COL,), OBS_DEV // 2, OBS_DEV + 1)
    full_holder = jax.random.randint(second, (), 0, N_COL)
    return jnp.where(jnp.arange(N_COL) == full_holder, OBS_DEV, counts).astype(jnp.int32)


def touch_ends(drawn, own_key, least, largest):
    extent = drawn.shape
    place = [jax.random.randint(jax.random.fold_in(own_key, axis), (), 0, extent[axis]) for axis in range(len(extent))]
    drawn = drawn.at[tuple(place)].set(least)
    longest = extent.index(max(extent))
    place[longest] = (place[longest] + 1) % extent[longest]
    return drawn.at[tuple(place)].set(largest)


def levels(key, extent, pieces, smallest, largest):
    loudness = 1.0
    for axis_at, parts in pieces:
        heights = jax.random.uniform(jax.random.fold_in(jax.random.fold_in(key, 6), axis_at), (parts,), jnp.float32, smallest / len(pieces), largest / len(pieces))
        loudness = loudness * jnp.repeat(jnp.exp(heights), extent[axis_at] // parts).reshape((-1,) + (1,) * (len(extent) - 1 - axis_at))
    return loudness


def routed_block(stream_key, own, number, rows, count, top, most, lean):
    sequence = jax.random.permutation(stream_key, count)
    packed, common = portions_of(count, rows * top, most, lean, True), portions_of(count, rows * top, most, lean, False)
    places = jnp.arange(count)

    def named(lengths, rotation):
        used = int((lengths > 0).sum())
        fixed = max(1, used // 4)
        shifted = fixed + (places - fixed + rotation * (used - fixed)) % max(1, count - fixed)
        return jnp.zeros((count,), jnp.int32).at[sequence[jnp.where(places < fixed, places, shifted)]].set(jnp.asarray(lengths, jnp.int32))

    lengths = jnp.where(number % 4 == 0, named(packed, number // 4), named(common, number - number // 4 - 1))
    mixed = jax.random.permutation(jax.random.fold_in(own, 3), count)
    giver, taker = mixed[0:count // 2 * 2:2], mixed[1:count // 2 * 2:2]
    room = jnp.minimum(lengths[giver] - 1, most - lengths[taker]) // 2
    room = jnp.where((giver == sequence[0]) | (taker == sequence[0]) | (lengths[taker] == 0), 0, jnp.maximum(room, 0))
    shifted = jax.random.randint(jax.random.fold_in(own, 4), (count // 2,), 0, 1 << 20) % (room + 1)
    lengths = lengths.at[giver].add(-shifted).at[taker].add(shifted)
    items = jnp.searchsorted(jnp.cumsum(lengths), jnp.arange(rows * top), side="right").astype(jnp.int32)
    listing = items.reshape(top, rows).T
    listing = listing[jax.random.permutation(jax.random.fold_in(own, 1), rows)]
    rotation = jax.random.randint(jax.random.fold_in(own, 2), (rows, 1), 0, top)
    return jnp.take_along_axis(listing, (jnp.arange(top)[None, :] + rotation) % top, axis=1)


def portions_of(count, total, bound, slope, full):
    loads = [(1 << 20) // math.isqrt(grade ** slope) + 1 for grade in range(1, count + 1)]
    largest = bound if full else min(bound, max(-(-total // count), total * loads[0] // sum(loads)))
    least = 1 if total - largest >= count - 1 else 0
    holding, rest = [largest] + [least] * (count - 1), total - largest - least * (count - 1)
    while rest > 0:
        free = [i for i in range(1, count) if holding[i] < largest] or [i for i in range(1, count) if holding[i] < bound]
        pool, left = sum([loads[i] for i in free]), rest
        for i in free:
            extra = min(bound - holding[i], max(1, left * loads[i] // pool), rest)
            holding[i] = holding[i] + extra
            rest = rest - extra
    return np.array(holding)


def normal_values(key, shape, scale, most, cuts=(), kind=jnp.bfloat16):
    entries = scale * jax.random.normal(key, shape, jnp.float32)
    if cuts:
        entries = entries * levels(key, shape, cuts, -0.22, 0.18)
    return jnp.clip(entries, -most, most).astype(kind)


def setup_inputs(seed: int = 0) -> dict:
    streams_of = jax.random.split(jax.random.key(seed), 10)
    perturbations = normal_values(streams_of[0], (MEMBERS, NY, NX, FEAT), 0.3, 4.0, ((0, 4), (1, 8)))
    static_root = draw_static_root(jax.random.fold_in(streams_of[9], 71), 0)
    obs_jacobian = normal_values(streams_of[2], (FEAT, CH), FEAT ** -0.5, 0.5, (), jnp.float32)
    innovations = normal_values(streams_of[3], (OBS_TOT, CH), 1.0, 6.0, ((0, 8),), jnp.float32)
    obs_weights = jnp.clip(jnp.exp(jax.random.uniform(streams_of[4], (CH,), jnp.float32, math.log(0.2), math.log(2.0))), 0.2, 2.0)
    length_scale = jnp.clip(0.05 + 0.19 * jax.random.uniform(streams_of[5], (NY, NX), jnp.float32) ** levels(streams_of[5], (NY, NX), ((0, 8),), -0.2, 0.2), 0.05, 0.24)
    obs_owner_keys = jax.random.split(jax.random.fold_in(streams_of[6], 1), OBS_TOT // OBS_DEV)
    obs_owner_turns = jax.random.permutation(jax.random.fold_in(streams_of[6], 3), OBS_TOT // OBS_DEV)
    obs_owner = jax.vmap(lambda own, number: routed_block(jax.random.fold_in(streams_of[6], 2), own, number, OBS_DEV, N_COL, 1, CAP, 2))(obs_owner_keys, obs_owner_turns).reshape((OBS_TOT, 1))
    obs_cell = touch_ends(jax.random.randint(streams_of[7], (OBS_TOT,), 0, CY * NX), jax.random.fold_in(streams_of[7], 1), 0, (CY * NX) - 1).astype(jnp.int32)
    obs_count = draw_obs_count(jax.random.fold_in(streams_of[9], 71), 0)
    return dict(perturbations=perturbations, static_root=static_root, obs_jacobian=obs_jacobian, innovations=innovations, obs_weights=obs_weights, length_scale=length_scale, obs_owner=obs_owner, obs_cell=obs_cell, obs_count=obs_count)


def face_coefficients(length_scale):
    padded = jnp.pad(length_scale, 1)
    return (jnp.sqrt(length_scale * padded[:-2, 1:-1]), jnp.sqrt(length_scale * padded[2:, 1:-1]), jnp.sqrt(length_scale * padded[1:-1, :-2]), jnp.sqrt(length_scale * padded[1:-1, 2:]))

def sweeps(values, coeffs):
    face_up, face_down, face_left, face_right = coeffs
    for sweep_step in range(NSWEEP):
        padded = jnp.pad(values, ((0, 0), (1, 1), (1, 1)))
        centre = values
        values = centre + face_up * (padded[:, :-2, 1:-1] - centre) + face_down * (padded[:, 2:, 1:-1] - centre) + face_left * (padded[:, 1:-1, :-2] - centre) + face_right * (padded[:, 1:-1, 2:] - centre)
    return values

def forward_map(perturbations, static_root, coeffs, static_part, ensemble_part):
    smoothed = lax.optimization_barrier(sweeps(ensemble_part, coeffs).astype(jnp.bfloat16))

    def add_member(total, pair):
        member, weight = pair
        return (total + member.astype(jnp.float32) * weight.astype(jnp.float32)[:, :, None], None)
    total, unused = lax.scan(add_member, jnp.zeros((NY, NX, FEAT), jnp.float32), (perturbations, smoothed))
    static = jnp.dot(static_part.reshape(NY * NX, FEAT), static_root, precision=lax.Precision.HIGHEST).reshape(NY, NX, FEAT)
    return total + static

def adjoint_map(perturbations, static_root, coeffs, gradient):
    static = jnp.dot(gradient.reshape(NY * NX, FEAT), static_root.T, precision=lax.Precision.HIGHEST).reshape(NY, NX, FEAT)
    rounded = lax.optimization_barrier(gradient.astype(jnp.bfloat16)).astype(jnp.float32)
    projected = lax.map(lambda member: lax.optimization_barrier(jnp.sum(member.astype(jnp.float32) * rounded, axis=-1)), perturbations)
    return (static, sweeps(projected, coeffs))

def reference(perturbations, static_root, obs_jacobian, innovations, obs_weights, length_scale, obs_owner, obs_cell, obs_count):
    coeffs = face_coefficients(length_scale)
    positions = jnp.arange(OBS_TOT, dtype=jnp.int32)
    live = (positions % OBS_DEV < obs_count[positions // OBS_DEV]).astype(jnp.float32)
    flat_index = (obs_owner[:, 0] * (CY * NX) + obs_cell).astype(jnp.int32)
    obs_gain = live[:, None] * obs_weights[None, :]

    def spread_back(weighted):
        back = jnp.dot(weighted, obs_jacobian.T, precision=lax.Precision.HIGHEST)
        return jnp.zeros((NY * NX, FEAT), jnp.float32).at[flat_index].add(back).reshape(NY, NX, FEAT)

    def obs_hessian(image_part):
        gathered = image_part.reshape(NY * NX, FEAT)[flat_index]
        model_obs = jnp.dot(gathered, obs_jacobian, precision=lax.Precision.HIGHEST)
        return spread_back(obs_gain * model_obs)

    def inner(first, second):
        return jnp.sum(first[0] * second[0]) + jnp.sum(first[1] * second[1])
    residual = adjoint_map(perturbations, static_root, coeffs, spread_back(obs_gain * innovations))
    direction = residual
    state = (jnp.zeros((NY, NX, FEAT), jnp.float32), jnp.zeros((MEMBERS, NY, NX), jnp.float32))
    increment = jnp.zeros((NY, NX, FEAT), jnp.float32)
    norm_now = inner(residual, residual)
    for iteration in range(ITERS):
        image_part = forward_map(perturbations, static_root, coeffs, direction[0], direction[1])
        adj_static, adj_ensemble = adjoint_map(perturbations, static_root, coeffs, obs_hessian(image_part))
        image = (direction[0] + adj_static, direction[1] + adj_ensemble)
        step = norm_now / inner(direction, image)
        state = (state[0] + step * direction[0], state[1] + step * direction[1])
        residual = (residual[0] - step * image[0], residual[1] - step * image[1])
        increment = increment + step * image_part
        norm_next = inner(residual, residual)
        ratio = norm_next / norm_now
        direction = (residual[0] + ratio * direction[0], residual[1] + ratio * direction[1])
        norm_now = norm_next
    return (increment, state[0], state[1])
```

```python
import functools

import jax
import jax.numpy as jnp
from jax import lax
from jax.experimental import pallas as pl
from jax.experimental.pallas import tpu as pltpu
from jax.sharding import PartitionSpec as P

NSWEEP = 4
F32 = jnp.float32
BF16 = jnp.bfloat16
MESH = pl.DeviceIdType.MESH
HIGH = lax.Precision.HIGHEST
OFFSETS = (-2, -1, 1, 2)
NT = (((1,), (1,)), ((), ()))


def loop(count, body):
    if count <= 16:
        for i in range(count):
            body(i)
    else:
        lax.fori_loop(0, count, lambda i, c: (body(i), c)[1], 0)


def iota(shape, dim):
    return lax.broadcasted_iota(jnp.int32, shape, dim)


def exact(a, b):
    return jnp.dot(a, b, precision=HIGH, preferred_element_type=F32)


def exact_t(a, b):
    return lax.dot_general(a, b, NT, precision=HIGH, preferred_element_type=F32)


def kernel(
    nm, nb, cap,
    pert_hbm, root_ref, jac_ref, innov_ref, weight_ref, scale_ref, owner_ref, cell_ref, count_ref,
    inc_ref, stat_ref, ens_ref,
    pert, outbox, inbox, scales, vert, left, right, centre, pbuf, gfull, fpart, fsend, frecv,
    sums_col, sums_mem, ens_b, ens_h, acc, wdiag,
    pert_sem, obs_send, obs_recv, ls_send, ls_recv, g_send, g_recv, p_send, p_recv,
    f_send, f_recv, sc_send, sc_recv, sm_send, sm_recv,
):
    mem = lax.axis_index("mem")
    col = lax.axis_index("col")
    members, rows, columns, feat = pert.shape
    obs_dev = innov_ref.shape[0]
    quarter = columns // nm
    own_cols = rows * quarter
    total_rows = 5 * rows
    half = 128
    nblk = columns // half

    load = pltpu.make_async_copy(pert_hbm, pert, pert_sem)
    load.start()

    for phase in range(2):
        for r in range(2 * rows):
            pbuf[phase, r] = jnp.zeros((members, columns), F32)
            pbuf[phase, 3 * rows + r] = jnp.zeros((members, columns), F32)
    scales[...] = jnp.zeros_like(scales)
    scales[2, 0:rows, :] = scale_ref[...]

    barrier = pltpu.get_barrier_semaphore()

    def greet_col(i):
        pl.semaphore_signal(
            barrier, inc=1, device_id={"col": lax.rem(col + i + 1, nb)}, device_id_type=MESH
        )

    loop(nb - 1, greet_col)
    for i in range(1, nm):
        pl.semaphore_signal(
            barrier, inc=1, device_id={"mem": lax.rem(mem + i, nm)}, device_id_type=MESH
        )

    owner = owner_ref[...]
    cell = cell_ref[...]
    lane = iota((1, obs_dev), 1)
    live = lane < count_ref[...]
    owner = jnp.where(live, owner, -1)
    held = (owner == iota((nb, obs_dev), 0)).astype(F32)
    before = (iota((obs_dev, obs_dev), 0) < iota((obs_dev, obs_dev), 1)).astype(F32).astype(BF16)
    earlier = jnp.dot(held.astype(BF16), before, preferred_element_type=F32)
    rank = jnp.sum(earlier * held, axis=0, keepdims=True)
    col_shift = columns.bit_length() - 1
    q_shift = quarter.bit_length() - 1
    grid_row = lax.shift_right_logical(cell, col_shift)
    part = lax.shift_right_logical(cell, q_shift) & (nm - 1)
    inner = cell & (quarter - 1)
    kind = iota((16, obs_dev), 0)
    facts = jnp.where(
        kind == 0, grid_row,
        jnp.where(kind == 1, part, jnp.where(kind == 2, inner, jnp.where(kind == 3, 1, 0))),
    ).astype(F32).astype(BF16)
    innov = innov_ref[...].astype(BF16)
    slot_id = iota((128, obs_dev), 0).astype(F32)

    def message(target, box, at):
        mine = jnp.where(owner == target, rank, -1.0)
        pick = (slot_id == mine).astype(F32).astype(BF16)
        box[at, 0:cap, :] = jnp.dot(
            pick[0:cap], innov, preferred_element_type=F32
        ).astype(BF16)
        box[at, cap:cap + 16, :] = lax.dot_general(
            facts, pick, NT, preferred_element_type=F32
        ).astype(BF16)

    def obs_copy(i):
        return pltpu.make_async_remote_copy(
            src_ref=outbox.at[i], dst_ref=inbox.at[i],
            send_sem=obs_send.at[i], recv_sem=obs_recv.at[i],
            device_id={"col": lax.rem(col + i, nb)}, device_id_type=MESH,
        )

    pl.semaphore_wait(barrier, nb - 1 + nm - 1)

    def halo_copy(buf_src, buf_dst, send, recv, o):
        return pltpu.make_async_remote_copy(
            src_ref=buf_src, dst_ref=buf_dst, send_sem=send.at[2 + o], recv_sem=recv.at[2 - o],
            device_id={"col": lax.rem(col + o + nb, nb)}, device_id_type=MESH,
        )

    def inside(o):
        return col + o < nb if o > 0 else col + o >= 0

    def ls_copy(o):
        return halo_copy(scales.at[2], scales.at[2 - o], ls_send, ls_recv, o)

    def each_halo(make, action):
        for o in OFFSETS:
            @pl.when(inside(o))
            def _(o=o):
                getattr(make(o), action)()

    def halo_wait(make_wait):
        for o in OFFSETS:
            @pl.when(inside(o))
            def _(o=o):
                make_wait(o)

    each_halo(ls_copy, "start")

    def send_obs(i):
        message(lax.rem(col + i + 1, nb), outbox, i + 1)
        obs_copy(i + 1).start()

    loop(nb - 1, send_obs)
    message(col, inbox, 0)

    def wait_ls(o):
        ls_copy(-o).wait_recv()

    halo_wait(wait_ls)

    first_lane = iota((members, columns), 1) == 0

    def scale_row(r):
        return jnp.broadcast_to(scales[r // rows, r % rows:r % rows + 1, :], (members, columns))

    for r in range(total_rows):
        here = scale_row(r)
        face = jnp.sqrt(here * pltpu.roll(here, 1, 1))
        face = jnp.where(first_lane, 0.0, face)
        left[r] = face
        right[r] = pltpu.roll(face, columns - 1, 1)
        if r < total_rows - 1:
            vert[r] = jnp.sqrt(here * scale_row(r + 1))
    for r in range(1, total_rows - 1):
        centre[r] = 1.0 - (vert[r - 1] + vert[r] + left[r] + right[r])

    def smooth(phase, keep):
        values = [pbuf[phase, r] for r in range(total_rows)]
        for s in range(2 * NSWEEP):
            new = list(values)
            for r in range(s + 1, total_rows - s - 1):
                a = values[r]
                new[r] = (
                    centre[r] * a + vert[r - 1] * values[r - 1] + vert[r] * values[r + 1]
                    + left[r] * pltpu.roll(a, 1, 1) + right[r] * pltpu.roll(a, columns - 1, 1)
                )
            values = new
            if s == NSWEEP - 1:
                for y in range(rows):
                    keep[y] = values[2 * rows + y]
        return [values[2 * rows + y] for y in range(rows)]

    diagonal = iota((half, half), 0) == iota((half, half), 1)

    def block(y, b):
        return pert[:, y, b * half:(b + 1) * half, :].reshape(members * half, feat)

    own_slice = pl.ds(pl.multiple_of(mem * quarter, quarter), quarter)

    def g_copy(phase, i):
        at = phase * nm + i
        return pltpu.make_async_remote_copy(
            src_ref=gfull.at[phase, :, own_slice, :], dst_ref=gfull.at[phase, :, own_slice, :],
            send_sem=g_send.at[at], recv_sem=g_recv.at[at],
            device_id={"mem": lax.rem(mem + i, nm)}, device_id_type=MESH,
        )

    def p_copy(phase, o):
        own = pbuf.at[phase, pl.ds(2 * rows, rows)]
        return pltpu.make_async_remote_copy(
            src_ref=own, dst_ref=pbuf.at[phase, pl.ds((2 - o) * rows, rows)],
            send_sem=p_send.at[phase * 5 + 2 + o], recv_sem=p_recv.at[phase * 5 + 2 - o],
            device_id={"col": lax.rem(col + o + nb, nb)}, device_id_type=MESH,
        )

    def f_copy(phase, i):
        at = phase * nm + i
        target = lax.rem(mem + i, nm)
        return pltpu.make_async_remote_copy(
            src_ref=fsend.at[
                phase, :, pl.ds(pl.multiple_of(target * quarter, quarter), quarter), :
            ],
            dst_ref=frecv.at[phase, i],
            send_sem=f_send.at[at], recv_sem=f_recv.at[at],
            device_id={"mem": target}, device_id_type=MESH,
        )

    def round_trip(phase, grad, keep):
        gfull[phase, :, own_slice, :] = grad.astype(BF16).reshape(rows, quarter, feat)
        for i in range(1, nm):
            g_copy(phase, i).start()
        static = exact_t(grad, root_ref[...])
        forward = exact(static, root_ref[...])
        if phase == 0:
            load.wait()
        for i in range(1, nm):
            g_copy(phase, i).wait_recv()
        for y in range(rows):
            for b in range(nblk):
                full = lax.dot_general(
                    block(y, b), gfull[phase, y, b * half:(b + 1) * half, :], NT,
                    preferred_element_type=F32,
                ).reshape(members, half, half)
                pbuf[phase, 2 * rows + y, :, b * half:(b + 1) * half] = jnp.sum(
                    jnp.where(diagonal[None], full, 0.0), axis=1
                )
        each_halo(lambda o: p_copy(phase, o), "start")
        halo_wait(lambda o: p_copy(phase, -o).wait_recv())
        weights = smooth(phase, keep)
        for b in range(nblk):
            for y in range(rows):
                line = weights[y][:, b * half:(b + 1) * half]
                for k in range(members):
                    wdiag[:, k * half:(k + 1) * half] = jnp.where(
                        diagonal, line[k:k + 1, :], 0.0
                    ).astype(BF16)
                piece = jnp.dot(wdiag[...], block(y, b), preferred_element_type=F32)
                fpart[y, b * half:(b + 1) * half, :] = piece
                fsend[phase, y, b * half:(b + 1) * half, :] = piece.astype(BF16)
        for i in range(1, nm):
            f_copy(phase, i).start()
        image = fpart[:, own_slice, :].reshape(own_cols, feat) + forward
        for i in range(1, nm):
            f_copy(phase, i).wait_recv()
            image = image + frecv[phase, i].astype(F32).reshape(own_cols, feat)
        return static, image

    place = iota((own_cols, cap), 0).astype(F32)
    ones = jnp.ones((cap, feat), BF16)
    acc[...] = jnp.zeros_like(acc)

    def gather_obs(i):
        told = inbox[i, cap:cap + 16, :].astype(F32)
        ours = (told[3:4] > 0.5) & (told[1:2] == mem.astype(F32))
        spot = jnp.where(ours, told[0:1] * quarter + told[2:3], -1.0)
        chosen = (place == spot[:, 0:cap]).astype(F32).astype(BF16)
        acc[0] += jnp.dot(chosen, inbox[i, 0:cap, :], preferred_element_type=F32)
        acc[1] += jnp.dot(chosen, ones, preferred_element_type=F32)

    gather_obs(0)

    def receive_obs(i):
        obs_copy(i + 1).wait_recv()
        gather_obs(i + 1)

    loop(nb - 1, receive_obs)
    gain = acc[1] * weight_ref[...]
    grad = exact_t(acc[0] * weight_ref[...], jac_ref[...])
    static_b, image_b = round_trip(0, grad, ens_b)
    model_b = exact(image_b, jac_ref[...])
    weighted = gain * model_b
    static_h, image_h = round_trip(1, exact_t(weighted, jac_ref[...]), ens_h)
    model_h = exact(image_h, jac_ref[...])

    def lanes(x):
        return jnp.sum(x, axis=0, keepdims=True)

    def pair(first, second, s_first, s_second):
        total = lanes(s_first * s_second)
        e = lanes(jnp.sum(first[...] * second[...], axis=0))
        for b in range(nblk):
            total = total + e[:, b * half:(b + 1) * half]
        return total

    line = iota((8, 128), 0)
    tile = jnp.zeros((8, 128), F32)
    for at, term in enumerate((
        pair(ens_b, ens_b, static_b, static_b),
        pair(ens_b, ens_h, static_b, static_h),
        pair(ens_h, ens_h, static_h, static_h),
        lanes(weighted * model_b),
        lanes(weighted * model_h),
        lanes(gain * model_h * model_h),
    )):
        tile = jnp.where(line == at, term, tile)
    sums_col[0] = tile

    def sc_copy(i):
        return pltpu.make_async_remote_copy(
            src_ref=sums_col.at[0], dst_ref=sums_col.at[i],
            send_sem=sc_send.at[i], recv_sem=sc_recv.at[i],
            device_id={"col": lax.rem(col + i, nb)}, device_id_type=MESH,
        )

    def sm_copy(i):
        return pltpu.make_async_remote_copy(
            src_ref=sums_mem.at[0], dst_ref=sums_mem.at[i],
            send_sem=sm_send.at[i], recv_sem=sm_recv.at[i],
            device_id={"mem": lax.rem(mem + i, nm)}, device_id_type=MESH,
        )

    loop(nb - 1, lambda i: sc_copy(i + 1).start())
    loop(nb - 1, lambda i: sc_copy(i + 1).wait_recv())
    sums_mem[0] = jnp.sum(sums_col[...], axis=0)
    for i in range(1, nm):
        sm_copy(i).start()
    for i in range(1, nm):
        sm_copy(i).wait_recv()
    sums = jnp.sum(jnp.sum(sums_mem[...], axis=0), axis=1, keepdims=True)
    bb, bh, hh, zbb, zbh, zhh = (sums[i:i + 1] for i in range(6))

    step = bb / (bb + bh)
    rest = 1.0 - step
    norm = rest * rest * bb - 2.0 * step * rest * bh + step * step * hh
    along = rest + norm / bb
    curve = (
        along * along * (bb + zbb) - 2.0 * along * step * (bh + zbh) + step * step * (hh + zhh)
    )
    later = norm / curve
    first = step + later * along
    second = -later * step
    inc_ref[...] = (first * image_b + second * image_h).reshape(inc_ref.shape)
    stat_ref[...] = (first * static_b + second * static_h).reshape(stat_ref.shape)
    for y in range(rows):
        ens_ref[:, y, :] = first * ens_b[y] + second * ens_h[y]

    loop(nb - 1, lambda i: obs_copy(i + 1).wait_send())
    loop(nb - 1, lambda i: sc_copy(i + 1).wait_send())
    halo_wait(lambda o: ls_copy(o).wait_send())
    for phase in range(2):
        halo_wait(lambda o: p_copy(phase, o).wait_send())
        for i in range(1, nm):
            g_copy(phase, i).wait_send()
            f_copy(phase, i).wait_send()
    for i in range(1, nm):
        sm_copy(i).wait_send()


def shards(
    perturbations, static_root, obs_jacobian, innovations, obs_weights, length_scale,
    obs_owner, obs_cell, obs_count,
):
    members, rows, columns, feat = perturbations.shape
    nm, nb = lax.axis_size("mem"), lax.axis_size("col")
    obs_dev = innovations.shape[0]
    cap = max(16, 2 * obs_dev // nb)
    quarter = columns // nm
    own_cols = rows * quarter
    total_rows = 5 * rows
    vmem = pl.BlockSpec(memory_space=pltpu.VMEM)
    dma = pltpu.SemaphoreType.DMA
    strip = pltpu.VMEM((total_rows, members, columns), F32)
    return pl.pallas_call(
        functools.partial(kernel, nm, nb, cap),
        out_shape=(
            jax.ShapeDtypeStruct((rows, quarter, feat), F32),
            jax.ShapeDtypeStruct((rows, quarter, feat), F32),
            jax.ShapeDtypeStruct((members, rows, columns), F32),
        ),
        in_specs=[pl.BlockSpec(memory_space=pl.ANY)] + [vmem] * 8,
        out_specs=(vmem,) * 3,
        scratch_shapes=[
            pltpu.VMEM(perturbations.shape, BF16),
            pltpu.VMEM((nb, cap + 16, feat), BF16),
            pltpu.VMEM((nb, cap + 16, feat), BF16),
            pltpu.VMEM((5, 8, columns), F32),
            strip, strip, strip, strip,
            pltpu.VMEM((2, total_rows, members, columns), F32),
            pltpu.VMEM((2, rows, columns, feat), BF16),
            pltpu.VMEM((rows, columns, feat), F32),
            pltpu.VMEM((2, rows, columns, feat), BF16),
            pltpu.VMEM((2, nm, rows, quarter, feat), BF16),
            pltpu.VMEM((nb, 8, 128), F32),
            pltpu.VMEM((nm, 8, 128), F32),
            pltpu.VMEM((rows, members, columns), F32),
            pltpu.VMEM((rows, members, columns), F32),
            pltpu.VMEM((2, own_cols, feat), F32),
            pltpu.VMEM((128, members * 128), BF16),
            dma,
            dma((nb,)), dma((nb,)),
            dma((5,)), dma((5,)),
            dma((2 * nm,)), dma((2 * nm,)),
            dma((10,)), dma((10,)),
            dma((2 * nm,)), dma((2 * nm,)),
            dma((nb,)), dma((nb,)),
            dma((nm,)), dma((nm,)),
        ],
        compiler_params=pltpu.CompilerParams(
            collective_id=0, has_side_effects=True, vmem_limit_bytes=40 * 1024 * 1024
        ),
    )(
        perturbations, static_root, obs_jacobian, innovations, obs_weights.reshape(1, -1),
        length_scale, obs_owner.reshape(1, -1), obs_cell.reshape(1, -1), obs_count.reshape(1, 1),
    )


def solution(mesh):
    placed = (
        P("mem", "col", None, None),
        P(),
        P(),
        P("col", None),
        P(),
        P("col", None),
        P("col", None),
        P("col"),
        P("col"),
    )
    return jax.shard_map(
        shards,
        mesh=mesh,
        in_specs=placed,
        out_specs=(P("col", "mem", None), P("col", "mem", None), P("mem", "col", None)),
        check_vma=False,
    )
```

```python
import functools

import jax
import jax.numpy as jnp
from jax import lax
from jax.experimental import pallas as pl
from jax.experimental.pallas import tpu as pltpu
from jax.sharding import PartitionSpec as P

NSWEEP = 4
F32 = jnp.float32
BF16 = jnp.bfloat16
MESH = pl.DeviceIdType.MESH
OFFSETS = (-2, -1, 1, 2)
NN = (((1,), (0,)), ((), ()))
NT = (((1,), (1,)), ((), ()))


def loop(count, body):
    if count <= 16:
        for i in range(count):
            body(i)
    else:
        lax.fori_loop(0, count, lambda i, c: (body(i), c)[1], 0)


def iota(shape, dim):
    return lax.broadcasted_iota(jnp.int32, shape, dim)


def halves(a):
    high = a.astype(BF16)
    return high, (a - high.astype(F32)).astype(BF16)


def product(a, b, dims):
    a_high, a_low = halves(a)
    b_high, b_low = halves(b)

    def dot(x, y):
        return lax.dot_general(x, y, dims, preferred_element_type=F32)

    return dot(a_high, b_high) + (dot(a_high, b_low) + dot(a_low, b_high))


def exact(a, b):
    return product(a, b, NN)


def exact_t(a, b):
    return product(a, b, NT)


def kernel(
    nm, nb, cap,
    pert_hbm, root_hbm, jac_hbm, innov_hbm, weight_hbm, scale_hbm, owner_hbm, cell_hbm, count_hbm,
    inc_ref, stat_ref, ens_ref,
    pert, root_ref, jac_ref, innov_ref, weight_ref, scale_ref, owner_ref, cell_ref, count_ref,
    outbox, inbox, scales, vert, left, right, centre, pbuf, gfull, fpart, fsend, frecv,
    sums_col, sums_mem, ens_b, ens_h, grads, counts, wdiag,
    load_sem, obs_send, obs_recv, ls_send, ls_recv, g_send, g_recv, p_send, p_recv,
    f_send, f_recv, sc_send, sc_recv, sm_send, sm_recv,
):
    mem = lax.axis_index("mem")
    col = lax.axis_index("col")
    members, rows, columns, feat = pert.shape
    obs_dev = innov_ref.shape[0]
    quarter = columns // nm
    own_cols = rows * quarter
    total_rows = 5 * rows
    half = 128
    nblk = columns // half

    loads = [
        pltpu.make_async_copy(source, target, load_sem.at[i])
        for i, (source, target) in enumerate((
            (owner_hbm, owner_ref), (cell_hbm, cell_ref), (count_hbm, count_ref),
            (scale_hbm, scale_ref), (innov_hbm, innov_ref), (weight_hbm, weight_ref),
            (jac_hbm, jac_ref), (root_hbm, root_ref), (pert_hbm, pert),
        ))
    ]
    for load in loads:
        load.start()

    for phase in range(2):
        for r in range(2 * rows):
            pbuf[phase, r] = jnp.zeros((members, columns), F32)
            pbuf[phase, 3 * rows + r] = jnp.zeros((members, columns), F32)
    scales[...] = jnp.zeros_like(scales)

    barrier = pltpu.get_barrier_semaphore()

    def greet_col(i):
        pl.semaphore_signal(
            barrier, inc=1, device_id={"col": lax.rem(col + i + 1, nb)}, device_id_type=MESH
        )

    loop(nb - 1, greet_col)
    for i in range(1, nm):
        pl.semaphore_signal(
            barrier, inc=1, device_id={"mem": lax.rem(mem + i, nm)}, device_id_type=MESH
        )

    for load in loads[:-1]:
        load.wait()
    scales[2, 0:rows, :] = scale_ref[...]

    owner = owner_ref[...]
    cell = cell_ref[...]
    lane = iota((1, obs_dev), 1)
    live = lane < count_ref[...]
    owner = jnp.where(live, owner, -1)
    held = (owner == iota((nb, obs_dev), 0)).astype(F32)
    before = (iota((obs_dev, obs_dev), 0) < iota((obs_dev, obs_dev), 1)).astype(F32).astype(BF16)
    earlier = jnp.dot(held.astype(BF16), before, preferred_element_type=F32)
    rank = jnp.sum(earlier * held, axis=0, keepdims=True)
    col_shift = columns.bit_length() - 1
    q_shift = quarter.bit_length() - 1
    grid_row = lax.shift_right_logical(cell, col_shift)
    part = lax.shift_right_logical(cell, q_shift) & (nm - 1)
    inner = cell & (quarter - 1)
    kind = iota((16, obs_dev), 0)
    facts = jnp.where(
        kind == 0, grid_row,
        jnp.where(kind == 1, part, jnp.where(kind == 2, inner, jnp.where(kind == 3, 1, 0))),
    ).astype(F32).astype(BF16)
    innov = jnp.concatenate(halves(innov_ref[...]), axis=1)
    slot_id = iota((128, obs_dev), 0).astype(F32)

    def message(target, box, at):
        mine = jnp.where(owner == target, rank, -1.0)
        pick = (slot_id == mine).astype(F32).astype(BF16)
        box[at, 0:cap, :] = jnp.dot(
            pick[0:cap], innov, preferred_element_type=F32
        ).astype(BF16)
        box[at, cap:cap + 16, 0:128] = lax.dot_general(
            facts, pick, NT, preferred_element_type=F32
        ).astype(BF16)
        box[at, cap:cap + 16, feat:2 * feat] = jnp.zeros((16, feat), BF16)

    def obs_copy(i):
        return pltpu.make_async_remote_copy(
            src_ref=outbox.at[i], dst_ref=inbox.at[i],
            send_sem=obs_send.at[i], recv_sem=obs_recv.at[i],
            device_id={"col": lax.rem(col + i, nb)}, device_id_type=MESH,
        )

    pl.semaphore_wait(barrier, nb - 1 + nm - 1)

    def halo_copy(buf_src, buf_dst, send, recv, o):
        return pltpu.make_async_remote_copy(
            src_ref=buf_src, dst_ref=buf_dst, send_sem=send.at[2 + o], recv_sem=recv.at[2 - o],
            device_id={"col": lax.rem(col + o + nb, nb)}, device_id_type=MESH,
        )

    def inside(o):
        return col + o < nb if o > 0 else col + o >= 0

    def ls_copy(o):
        return halo_copy(scales.at[2], scales.at[2 - o], ls_send, ls_recv, o)

    def each_halo(make, action):
        for o in OFFSETS:
            @pl.when(inside(o))
            def _(o=o):
                getattr(make(o), action)()

    def halo_wait(make_wait):
        for o in OFFSETS:
            @pl.when(inside(o))
            def _(o=o):
                make_wait(o)

    each_halo(ls_copy, "start")

    def send_obs(i):
        message(lax.rem(col + i + 1, nb), outbox, i + 1)
        obs_copy(i + 1).start()

    loop(nb - 1, send_obs)
    message(col, inbox, 0)

    def wait_ls(o):
        ls_copy(-o).wait_recv()

    halo_wait(wait_ls)

    first_lane = iota((members, columns), 1) == 0

    def scale_row(r):
        return jnp.broadcast_to(scales[r // rows, r % rows:r % rows + 1, :], (members, columns))

    for r in range(total_rows):
        here = scale_row(r)
        face = jnp.sqrt(here * pltpu.roll(here, 1, 1))
        face = jnp.where(first_lane, 0.0, face)
        left[r] = face
        right[r] = pltpu.roll(face, columns - 1, 1)
        if r < total_rows - 1:
            vert[r] = jnp.sqrt(here * scale_row(r + 1))
    for r in range(1, total_rows - 1):
        centre[r] = 1.0 - (vert[r - 1] + vert[r] + left[r] + right[r])

    def smooth(phase, keep):
        values = [pbuf[phase, r] for r in range(total_rows)]
        for s in range(2 * NSWEEP):
            new = list(values)
            for r in range(s + 1, total_rows - s - 1):
                a = values[r]
                new[r] = (
                    centre[r] * a + vert[r - 1] * values[r - 1] + vert[r] * values[r + 1]
                    + left[r] * pltpu.roll(a, 1, 1) + right[r] * pltpu.roll(a, columns - 1, 1)
                )
            values = new
            if s == NSWEEP - 1:
                for y in range(rows):
                    keep[y] = values[2 * rows + y]
        return [values[2 * rows + y] for y in range(rows)]

    diagonal = iota((half, half), 0) == iota((half, half), 1)

    def block(y, b):
        return pert[:, y, b * half:(b + 1) * half, :].reshape(members * half, feat)

    own_slice = pl.ds(pl.multiple_of(mem * quarter, quarter), quarter)

    def g_copy(phase, i):
        at = phase * nm + i
        return pltpu.make_async_remote_copy(
            src_ref=gfull.at[phase, :, own_slice, :], dst_ref=gfull.at[phase, :, own_slice, :],
            send_sem=g_send.at[at], recv_sem=g_recv.at[at],
            device_id={"mem": lax.rem(mem + i, nm)}, device_id_type=MESH,
        )

    def p_copy(phase, o):
        own = pbuf.at[phase, pl.ds(2 * rows, rows)]
        return pltpu.make_async_remote_copy(
            src_ref=own, dst_ref=pbuf.at[phase, pl.ds((2 - o) * rows, rows)],
            send_sem=p_send.at[phase * 5 + 2 + o], recv_sem=p_recv.at[phase * 5 + 2 - o],
            device_id={"col": lax.rem(col + o + nb, nb)}, device_id_type=MESH,
        )

    def f_copy(phase, i):
        at = phase * nm + i
        target = lax.rem(mem + i, nm)
        return pltpu.make_async_remote_copy(
            src_ref=fsend.at[
                phase, :, pl.ds(pl.multiple_of(target * quarter, quarter), quarter), :
            ],
            dst_ref=frecv.at[phase, i],
            send_sem=f_send.at[at], recv_sem=f_recv.at[at],
            device_id={"mem": target}, device_id_type=MESH,
        )

    def round_trip(phase, grad, keep):
        if phase > 0:
            gfull[phase, :, own_slice, :] = grad.astype(BF16).reshape(rows, quarter, feat)
            for i in range(1, nm):
                g_copy(phase, i).start()
        static = exact_t(grad, root_ref[...])
        forward = exact(static, root_ref[...])
        if phase == 0:
            loads[-1].wait()
        if phase > 0:
            for i in range(1, nm):
                g_copy(phase, i).wait_recv()
        for y in range(rows):
            for b in range(nblk):
                full = lax.dot_general(
                    block(y, b), gfull[phase, y, b * half:(b + 1) * half, :], NT,
                    preferred_element_type=F32,
                ).reshape(members, half, half)
                pbuf[phase, 2 * rows + y, :, b * half:(b + 1) * half] = jnp.sum(
                    jnp.where(diagonal[None], full, 0.0), axis=1
                )
        each_halo(lambda o: p_copy(phase, o), "start")
        halo_wait(lambda o: p_copy(phase, -o).wait_recv())
        weights = smooth(phase, keep)
        for b in range(nblk):
            for y in range(rows):
                line = weights[y][:, b * half:(b + 1) * half]
                for k in range(members):
                    wdiag[:, k * half:(k + 1) * half] = jnp.where(
                        diagonal, line[k:k + 1, :], 0.0
                    ).astype(BF16)
                piece = jnp.dot(wdiag[...], block(y, b), preferred_element_type=F32)
                fpart[y, b * half:(b + 1) * half, :] = piece
                fsend[phase, y, b * half:(b + 1) * half, :] = piece.astype(BF16)
            for i in range(1, nm):
                @pl.when(lax.rem(mem + i, nm) * quarter // half == b)
                def _(i=i):
                    f_copy(phase, i).start()
        image = fpart[:, own_slice, :].reshape(own_cols, feat) + forward
        for i in range(1, nm):
            f_copy(phase, i).wait_recv()
            image = image + frecv[phase, i].astype(F32).reshape(own_cols, feat)
        return static, image

    gain_map = exact_t(jac_ref[...] * weight_ref[...], jac_ref[...])
    loop(nb - 1, lambda i: obs_copy(i + 1).wait_recv())
    slots = nb * cap
    told = jnp.concatenate(
        [inbox[i, cap:cap + 16, 0:128].astype(F32)[:, 0:cap] for i in range(nb)], axis=1
    )
    spot = (told[0:1] * nm + told[1:2]) * quarter + told[2:3]
    spot = jnp.where(told[3:4] > 0.5, spot, -1.0)
    sent = jnp.concatenate(
        [inbox[:, 0:cap, :].reshape(slots, 2 * feat), jnp.ones((slots, feat), BF16)], axis=1
    )
    place = iota((columns, slots), 0).astype(F32)
    for y in range(rows):
        chosen = (place == spot - y * columns).astype(F32).astype(BF16)
        found = jnp.dot(chosen, sent, preferred_element_type=F32)
        counts[y] = found[:, 2 * feat:]
        total = (found[:, :feat] + found[:, feat:2 * feat]) * weight_ref[...]
        row_grad = exact_t(total, jac_ref[...])
        grads[y] = row_grad
        gfull[0, y] = row_grad.astype(BF16)
    grad = grads[:, own_slice, :].reshape(own_cols, feat)
    count = counts[:, own_slice, :].reshape(own_cols, feat)
    static_b, image_b = round_trip(0, grad, ens_b)
    back_b = count * exact(image_b, gain_map)
    static_h, image_h = round_trip(1, back_b, ens_h)
    back_h = count * exact(image_h, gain_map)

    def lanes(x):
        return jnp.sum(x, axis=0, keepdims=True)

    def pair(first, second, s_first, s_second):
        total = lanes(s_first * s_second)
        e = lanes(jnp.sum(first[...] * second[...], axis=0))
        for b in range(nblk):
            total = total + e[:, b * half:(b + 1) * half]
        return total

    line = iota((8, 128), 0)
    tile = jnp.zeros((8, 128), F32)
    for at, term in enumerate((
        pair(ens_b, ens_b, static_b, static_b),
        pair(ens_b, ens_h, static_b, static_h),
        pair(ens_h, ens_h, static_h, static_h),
        lanes(image_b * back_b),
        lanes(image_h * back_b),
        lanes(image_h * back_h),
    )):
        tile = jnp.where(line == at, term, tile)
    sums_col[0] = tile

    def sc_copy(i):
        return pltpu.make_async_remote_copy(
            src_ref=sums_col.at[0], dst_ref=sums_col.at[i],
            send_sem=sc_send.at[i], recv_sem=sc_recv.at[i],
            device_id={"col": lax.rem(col + i, nb)}, device_id_type=MESH,
        )

    def sm_copy(i):
        return pltpu.make_async_remote_copy(
            src_ref=sums_mem.at[0], dst_ref=sums_mem.at[i],
            send_sem=sm_send.at[i], recv_sem=sm_recv.at[i],
            device_id={"mem": lax.rem(mem + i, nm)}, device_id_type=MESH,
        )

    loop(nb - 1, lambda i: sc_copy(i + 1).start())
    loop(nb - 1, lambda i: sc_copy(i + 1).wait_recv())
    sums_mem[0] = jnp.sum(sums_col[...], axis=0)
    for i in range(1, nm):
        sm_copy(i).start()
    for i in range(1, nm):
        sm_copy(i).wait_recv()
    sums = jnp.sum(jnp.sum(sums_mem[...], axis=0), axis=1, keepdims=True)
    bb, bh, hh, zbb, zbh, zhh = (sums[i:i + 1] for i in range(6))

    step = bb / (bb + bh)
    rest = 1.0 - step
    norm = rest * rest * bb - 2.0 * step * rest * bh + step * step * hh
    along = rest + norm / bb
    curve = (
        along * along * (bb + zbb) - 2.0 * along * step * (bh + zbh) + step * step * (hh + zhh)
    )
    later = norm / curve
    first = step + later * along
    second = -later * step
    inc_ref[...] = (first * image_b + second * image_h).reshape(inc_ref.shape)
    stat_ref[...] = (first * static_b + second * static_h).reshape(stat_ref.shape)
    for y in range(rows):
        ens_ref[:, y, :] = first * ens_b[y] + second * ens_h[y]

    loop(nb - 1, lambda i: obs_copy(i + 1).wait_send())
    loop(nb - 1, lambda i: sc_copy(i + 1).wait_send())
    halo_wait(lambda o: ls_copy(o).wait_send())
    for phase in range(2):
        halo_wait(lambda o: p_copy(phase, o).wait_send())
        for i in range(1, nm):
            if phase > 0:
                g_copy(phase, i).wait_send()
            f_copy(phase, i).wait_send()
    for i in range(1, nm):
        sm_copy(i).wait_send()


def shards(
    perturbations, static_root, obs_jacobian, innovations, obs_weights, length_scale,
    obs_owner, obs_cell, obs_count,
):
    members, rows, columns, feat = perturbations.shape
    nm, nb = lax.axis_size("mem"), lax.axis_size("col")
    obs_dev = innovations.shape[0]
    cap = max(16, 2 * obs_dev // nb)
    quarter = columns // nm
    total_rows = 5 * rows
    vmem = pl.BlockSpec(memory_space=pltpu.VMEM)
    dma = pltpu.SemaphoreType.DMA
    strip = pltpu.VMEM((total_rows, members, columns), F32)
    return pl.pallas_call(
        functools.partial(kernel, nm, nb, cap),
        out_shape=(
            jax.ShapeDtypeStruct((rows, quarter, feat), F32),
            jax.ShapeDtypeStruct((rows, quarter, feat), F32),
            jax.ShapeDtypeStruct((members, rows, columns), F32),
        ),
        in_specs=[pl.BlockSpec(memory_space=pltpu.HBM)] * 9,
        out_specs=(vmem,) * 3,
        scratch_shapes=[
            pltpu.VMEM(perturbations.shape, BF16),
            pltpu.VMEM(static_root.shape, F32),
            pltpu.VMEM(obs_jacobian.shape, F32),
            pltpu.VMEM(innovations.shape, F32),
            pltpu.VMEM((1, feat), F32),
            pltpu.VMEM(length_scale.shape, F32),
            pltpu.VMEM((1, obs_dev), jnp.int32),
            pltpu.VMEM((1, obs_dev), jnp.int32),
            pltpu.VMEM((1, 1), jnp.int32),
            pltpu.VMEM((nb, cap + 16, 2 * feat), BF16),
            pltpu.VMEM((nb, cap + 16, 2 * feat), BF16),
            pltpu.VMEM((5, 8, columns), F32),
            strip, strip, strip, strip,
            pltpu.VMEM((2, total_rows, members, columns), F32),
            pltpu.VMEM((2, rows, columns, feat), BF16),
            pltpu.VMEM((rows, columns, feat), F32),
            pltpu.VMEM((2, rows, columns, feat), BF16),
            pltpu.VMEM((2, nm, rows, quarter, feat), BF16),
            pltpu.VMEM((nb, 8, 128), F32),
            pltpu.VMEM((nm, 8, 128), F32),
            pltpu.VMEM((rows, members, columns), F32),
            pltpu.VMEM((rows, members, columns), F32),
            pltpu.VMEM((rows, columns, feat), F32),
            pltpu.VMEM((rows, columns, feat), F32),
            pltpu.VMEM((128, members * 128), BF16),
            dma((9,)),
            dma((nb,)), dma((nb,)),
            dma((5,)), dma((5,)),
            dma((2 * nm,)), dma((2 * nm,)),
            dma((10,)), dma((10,)),
            dma((2 * nm,)), dma((2 * nm,)),
            dma((nb,)), dma((nb,)),
            dma((nm,)), dma((nm,)),
        ],
        compiler_params=pltpu.CompilerParams(
            collective_id=0, has_side_effects=True, vmem_limit_bytes=62 * 1024 * 1024
        ),
    )(
        perturbations, static_root, obs_jacobian, innovations, obs_weights.reshape(1, -1),
        length_scale, obs_owner.reshape(1, -1), obs_cell.reshape(1, -1), obs_count.reshape(1, 1),
    )


def solution(mesh):
    placed = (
        P("mem", "col", None, None),
        P(),
        P(),
        P("col", None),
        P(),
        P("col", None),
        P("col", None),
        P("col"),
        P("col"),
    )
    return jax.shard_map(
        shards,
        mesh=mesh,
        in_specs=placed,
        out_specs=(P("col", "mem", None), P("col", "mem", None), P("mem", "col", None)),
        check_vma=False,
    )
```
